32 devices in a mesh: group: 2 (over y), region: 4 (over z), hid: 2 (over x), sub: 2 (over core).
Axes of the slice: x: 2, y: 2, z: 4, core: 2. Of those that a mesh axis runs over, the one named last changes fastest.
Arguments:
- edge_lat: bfloat16 [40960, 512], P(('group', 'region', 'sub')), parts along dimension 0, may hold values from -6 to 6
- node_lat: bfloat16 [4096, 512], P(('group', 'region', 'sub')), parts along dimension 0, may hold values from -6 to 6
- senders: int32 [40960], P(('group', 'region', 'sub')), parts along dimension 0, may hold values from 0 to 511
- recv_slots: int32 [40960], P(('group', 'region', 'sub')), parts along dimension 0, may hold values from 0 to 127
- owners: int32 [320, 1], P(('group', 'region', 'sub')), parts along dimension 0, may hold values from 0 to 3; in each aligned block of 20 rows (0 to 19, 20 to 39, ...) at most 7 rows name the same one
- targets: int32 [320], P(('group', 'region', 'sub')), parts along dimension 0, may hold values from 0 to 1
- w_edge_in: bfloat16 [1024, 512], P(None, 'hid'), may hold values from -0.1875 to 0.1875
- b_edge: bfloat16 [512], P('hid'), may hold values from -3 to 3
- w_edge_out: bfloat16 [512, 512], P('hid'), may hold values from -0.25 to 0.25
- w_node_in: bfloat16 [1024, 512], P(None, 'hid'), may hold values from -0.1875 to 0.1875
- b_node: bfloat16 [512], P('hid'), may hold values from -3 to 3
- w_node_out: bfloat16 [512, 512], P('hid'), may hold values from -0.25 to 0.25
- norm_gain: bfloat16 [512], replicated, may hold values from 0.099609375 to 1.8984375
- cotangent: bfloat16 [4096, 512], P(('group', 'region', 'sub')), parts along dimension 0, may hold values from -6 to 6
Outputs:
- new_nodes: bfloat16 [4096, 512], P(('group', 'region', 'sub')), parts along dimension 0
- grad_nodes: bfloat16 [4096, 512], P(('group', 'region', 'sub')), parts along dimension 0
- grad_edge_in: float32 [2048, 512], P('group', 'hid'), parts along dimension 0
- grad_edge_out: float32 [1024, 512], P(('group', 'hid')), parts along dimension 0
- grad_node_in: float32 [2048, 512], P('group', 'hid'), parts along dimension 0
- grad_node_out: float32 [1024, 512], P(('group', 'hid')), parts along dimension 0
The draws below stay inside these ranges and needn't reach their ends.
There are 2 independent parts, one for each index of `group`. The reference program is written for one: setup_inputs(seed, part) draws one part's arguments, and reference() takes and returns one part's arrays. A program takes and returns all parts, laid end to end along the dimension named above; an argument that names none is the same for every part. Nothing has to cross between parts.
Inputs may be any that keep to these rules, and one draw needn't show every extreme that they name: `owners`: among the 20 blocks of one index of region and sub, no region is named by more than 7 blocks, a bound that some block reaches of them in every draw.
All inputs are finite; a program needn't handle non-finite values.
Results may differ from the reference program's by a relative error of at most 0.023.
Values may be sent and summed in bfloat16 or wider, within the bound.
A program may use at most 128 MiB of HBM per device.

```python
import math
import jax
import jax.numpy as jnp
import numpy as np
from jax import lax

L = 512
H = 512
BLK = 128
EB_DEV = 20
RB = 2
CAP = 7
NODE_DEV = 256
NODES = 2048
BLOCKS = 160
EDGES = 20480
N_REGION = 4
N_HID = 2
N_SUB = 2


def plant(entries, key, least, largest):
    index_at = [jax.random.randint(jax.random.fold_in(key, axis), (), 0, length) for axis, length in enumerate(entries.shape)]
    main_axis = entries.shape.index(max(entries.shape))
    next_to = index_at[:main_axis] + [(index_at[main_axis] + 1) % entries.shape[main_axis]] + index_at[main_axis + 1:]
    return entries.at[tuple(index_at)].set(least).at[tuple(next_to)].set(largest)


def levels(key, shape, cuts, smallest, high):
    loudness, own = 1.0, jax.random.fold_in(key, 6)
    for dim, shards_of in cuts:
        heights = jnp.exp(jax.random.uniform(jax.random.fold_in(own, dim), (shards_of,), jnp.float32, smallest / len(cuts), high / len(cuts)))
        loudness = loudness * jnp.repeat(heights, shape[dim] // shards_of).reshape([-1 if axis == dim else 1 for axis in range(len(shape))])
    return loudness


def deal_out(own_key, own, number, rows, count, top, most, skew):
    order = jax.random.permutation(own_key, count)
    crowded, usual = shares(count, rows * top, most, skew, True), shares(count, rows * top, most, skew, False)
    places = jnp.arange(count)

    def named(sizes, turn):
        used = int((sizes > 0).sum())
        fixed = max(1, used // 4)
        passed = fixed + (places - fixed + turn * (used - fixed)) % max(1, count - fixed)
        return jnp.zeros((count,), jnp.int32).at[order[jnp.where(places < fixed, places, passed)]].set(jnp.asarray(sizes, jnp.int32))

    sizes = jnp.where(number % 4 == 0, named(crowded, number // 4), named(usual, number - number // 4 - 1))
    mixed = jax.random.permutation(jax.random.fold_in(own, 3), count)
    donor, receiver = mixed[0:count // 2 * 2:2], mixed[1:count // 2 * 2:2]
    slack = jnp.minimum(sizes[donor] - 1, most - sizes[receiver]) // 2
    slack = jnp.where((donor == order[0]) | (receiver == order[0]) | (sizes[receiver] == 0), 0, jnp.maximum(slack, 0))
    passed = jax.random.randint(jax.random.fold_in(own, 4), (count // 2,), 0, 1 << 20) % (slack + 1)
    sizes = sizes.at[donor].add(-passed).at[receiver].add(passed)
    items = jnp.searchsorted(jnp.cumsum(sizes), jnp.arange(rows * top), side="right").astype(jnp.int32)
    listing = items.reshape(top, rows).T
    listing = listing[jax.random.permutation(jax.random.fold_in(own, 1), rows)]
    turn = jax.random.randint(jax.random.fold_in(own, 2), (rows, 1), 0, top)
    return jnp.take_along_axis(listing, (jnp.arange(top)[None, :] + turn) % top, axis=1)


def shares(number_of, total, bound, skew, full):
    loads = [(1 << 20) // math.isqrt(grade ** skew) + 1 for grade in range(1, number_of + 1)]
    largest = bound if full else min(bound, max(-(-total // number_of), total * loads[0] // sum(loads)))
    least = 1 if total - largest >= number_of - 1 else 0
    holding, rest = [largest] + [least] * (number_of - 1), total - largest - least * (number_of - 1)
    while rest > 0:
        candidates = [i for i in range(1, number_of) if holding[i] < largest] or [i for i in range(1, number_of) if holding[i] < bound]
        mass, budget = sum([loads[i] for i in candidates]), rest
        for i in candidates:
            extra = min(bound - holding[i], max(1, budget * loads[i] // mass), rest)
            holding[i] = holding[i] + extra
            rest = rest - extra
    return np.array(holding)


def normal_values(stream_key, extent, scale, limit, pieces=(), kind=jnp.bfloat16):
    factor_of = levels(stream_key, extent, pieces, -0.22, 0.18) if pieces else 1.0
    drawn = jax.random.normal(stream_key, extent, jnp.float32) * scale * factor_of
    return jnp.minimum(jnp.maximum(drawn, -limit), limit).astype(kind)


def setup_inputs(seed: int = 0, part: int = 0) -> dict:
    seeds = jax.random.split(jax.random.key(seed), 15)
    own_keys = jax.random.split(jax.random.fold_in(seeds[14], part), 15)
    edge_lat = normal_values(own_keys[0], (EDGES, L), 1.0, 6.0, ((0, 8),))
    node_lat = normal_values(own_keys[1], (NODES, L), 1.0, 6.0, ((0, 8),))
    senders = plant(jax.random.randint(own_keys[2], (EDGES,), 0, N_SUB * NODE_DEV), jax.random.fold_in(own_keys[2], 1), 0, (N_SUB * NODE_DEV) - 1).astype(jnp.int32)
    recv_slots = plant(jax.random.randint(own_keys[3], (EDGES,), 0, BLK), jax.random.fold_in(own_keys[3], 1), 0, BLK - 1).astype(jnp.int32)
    owners_keys = jax.random.split(jax.random.fold_in(own_keys[4], 1), BLOCKS // EB_DEV)
    owners_turns = jax.random.permutation(jax.random.fold_in(own_keys[4], 3), BLOCKS // EB_DEV)
    owners = jax.vmap(lambda own, number: deal_out(jax.random.fold_in(own_keys[4], 2), own, number, EB_DEV, N_REGION, 1, CAP, 2))(owners_keys, owners_turns).reshape((BLOCKS, 1))
    targets = plant(jax.random.randint(own_keys[5], (BLOCKS,), 0, RB), jax.random.fold_in(own_keys[5], 1), 0, RB - 1).astype(jnp.int32)
    w_edge_in = normal_values(seeds[6], (2 * L, H), (2 * L) ** -0.5, 0.1875, ((1, 2),))
    b_edge = normal_values(seeds[7], (H,), 0.5, 3.0, ((0, 2),))
    w_edge_out = normal_values(seeds[8], (H, L), H ** -0.5, 0.25, ((0, 2),))
    w_node_in = normal_values(seeds[9], (2 * L, H), (2 * L) ** -0.5, 0.1875, ((1, 2),))
    b_node = normal_values(seeds[10], (H,), 0.5, 3.0, ((0, 2),))
    w_node_out = normal_values(seeds[11], (H, L), H ** -0.5, 0.25, ((0, 2),))
    norm_gain = jnp.clip(1.0 + 0.18 * jax.random.normal(seeds[12], (L,), jnp.float32), 0.099609375, 1.8984375).astype(jnp.bfloat16)
    cotangent = normal_values(own_keys[13], (NODES, L), 1.0, 6.0, ((0, 8),))
    return dict(edge_lat=edge_lat, node_lat=node_lat, senders=senders, recv_slots=recv_slots, owners=owners, targets=targets, w_edge_in=w_edge_in, b_edge=b_edge, w_edge_out=w_edge_out, w_node_in=w_node_in, b_node=b_node, w_node_out=w_node_out, norm_gain=norm_gain, cotangent=cotangent)


def silu_slope(values):
    logistic = jax.nn.sigmoid(values)
    return logistic * (1.0 + values * (1.0 - logistic))

def layer_norm(values, norm_gain):
    row_mean = lax.optimization_barrier(jnp.mean(values, axis=-1, keepdims=True))
    centred = values - row_mean
    spread = lax.optimization_barrier(jnp.mean(centred * centred, axis=-1, keepdims=True))
    return centred * lax.rsqrt(spread + 1e-05) * norm_gain

def reference(edge_lat, node_lat, senders, recv_slots, owners, targets, w_edge_in, b_edge, w_edge_out, w_node_in, b_node, w_node_out, norm_gain, cotangent):
    recv_rows = RB * BLK
    edge_index = jnp.arange(EDGES, dtype=jnp.int32)
    edge_device = edge_index // (EB_DEV * BLK)
    edge_region = edge_device // N_SUB
    sender_global = edge_region * (N_SUB * recv_rows) + senders
    inputs = jnp.concatenate([edge_lat, node_lat[sender_global]], axis=1)
    edge_pre = jnp.dot(inputs, w_edge_in, preferred_element_type=jnp.float32) + b_edge.astype(jnp.float32)
    hidden = jax.nn.silu(edge_pre).astype(jnp.bfloat16)
    edge_cell = edge_index // BLK * BLK + recv_slots
    summed = jax.ops.segment_sum(hidden.astype(jnp.float32), edge_cell, num_segments=BLOCKS * BLK).astype(jnp.bfloat16)
    block_index = jnp.arange(BLOCKS, dtype=jnp.int32)
    dest_device = owners[:, 0] * N_SUB + block_index // EB_DEV % N_SUB
    node_of_row = (dest_device * recv_rows + targets * BLK)[:, None] + jnp.arange(BLK, dtype=jnp.int32)[None, :]
    node_of_row = node_of_row.reshape(-1)
    hid_width = H // N_HID

    def add_share(running, hid_share):
        first_col = (hid_share * hid_width).astype(jnp.int32)
        hid_piece = lax.dynamic_slice_in_dim(summed, first_col, hid_width, 1)
        weight = lax.dynamic_slice_in_dim(w_edge_out, first_col, hid_width, 0)
        hid_part = jnp.dot(hid_piece, weight, preferred_element_type=jnp.float32).astype(jnp.bfloat16)
        return (running + jax.ops.segment_sum(hid_part.astype(jnp.float32), node_of_row, num_segments=NODES), None)
    gathered, _ = lax.scan(add_share, jnp.zeros((NODES, L), jnp.float32), jnp.arange(N_HID, dtype=jnp.int32))
    node_in = jnp.concatenate([node_lat, gathered.astype(jnp.bfloat16)], axis=1)
    node_pre = jnp.dot(node_in, w_node_in, preferred_element_type=jnp.float32) + b_node.astype(jnp.float32)
    node_hidden = jax.nn.silu(node_pre).astype(jnp.bfloat16)
    update = jnp.dot(node_hidden, w_node_out, preferred_element_type=jnp.float32)
    gain_values = norm_gain.astype(jnp.float32)
    normed, norm_back = jax.vjp(lambda values: layer_norm(values, gain_values), update)
    new_nodes = (node_lat.astype(jnp.float32) + normed).astype(jnp.bfloat16)
    grad_update = norm_back(cotangent.astype(jnp.float32))[0].astype(jnp.bfloat16)
    grad_node_out = jnp.dot(node_hidden.T, grad_update, preferred_element_type=jnp.float32)
    grad_node_pre = (jnp.dot(grad_update, w_node_out.T, preferred_element_type=jnp.float32) * silu_slope(node_pre)).astype(jnp.bfloat16)
    grad_node_in = jnp.dot(node_in.T, grad_node_pre, preferred_element_type=jnp.float32)
    grad_node_cat = jnp.dot(grad_node_pre, w_node_in.T, preferred_element_type=jnp.float32)
    grad_gathered = grad_node_cat[:, L:].astype(jnp.bfloat16)
    grad_rows = grad_gathered[node_of_row]
    grad_summed = jnp.dot(grad_rows, w_edge_out.T, preferred_element_type=jnp.float32).astype(jnp.bfloat16)
    grad_edge_out = jnp.dot(summed.T, grad_rows, preferred_element_type=jnp.float32)
    grad_pre = (grad_summed[edge_cell].astype(jnp.float32) * silu_slope(edge_pre)).astype(jnp.bfloat16)
    grad_edge_in = jnp.dot(inputs.T, grad_pre, preferred_element_type=jnp.float32)
    grad_send = jnp.dot(grad_pre, w_edge_in[L:].T, preferred_element_type=jnp.float32)
    sender_part = jax.ops.segment_sum(grad_send, sender_global, num_segments=NODES)
    grad_nodes = (cotangent.astype(jnp.float32) + grad_node_cat[:, :L] + sender_part).astype(jnp.bfloat16)
    return (new_nodes, grad_nodes, grad_edge_in, grad_edge_out, grad_node_in, grad_node_out)
```

```python
import functools
import jax
import jax.numpy as jnp
from jax import lax
from jax.experimental import pallas as pl
from jax.experimental.pallas import tpu as pltpu
from jax.sharding import PartitionSpec as P

F32 = jnp.float32
BF16 = jnp.bfloat16
MESH = pl.DeviceIdType.MESH
VMEM_BYTES = 48 * 1024 * 1024


def dot(a, b):
    return jnp.dot(a, b, preferred_element_type=F32)


def dot_t(a, b):
    return lax.dot_general(a, b, (((1,), (1,)), ((), ())), preferred_element_type=F32)


def t_dot(a, b):
    return lax.dot_general(a, b, (((0,), (0,)), ((), ())), preferred_element_type=F32)


def logistic(v):
    return 1.0 / (1.0 + jnp.exp(-v))


def edge_forward_kernel(
    block_rows, per_step, codes, lat, send, slot, own_part, other_part, w_lat, bias, agg, slope, total
):
    step = pl.program_id(0)
    edges = lat.shape[0]
    nodes = own_part.shape[0]

    @pl.when(step == 0)
    def _():
        total[...] = jnp.zeros_like(total)

    places = lax.broadcasted_iota(jnp.int32, (nodes, edges), 0)
    ids = send[0]
    pre = dot(lat[...], w_lat[...]) + bias[...].astype(F32)
    pre += t_dot((places == ids).astype(BF16), own_part[...])
    pre += t_dot((places + nodes == ids).astype(BF16), other_part[...])
    gate = logistic(pre)
    hidden = (pre * gate).astype(BF16)
    slope[...] = (gate * (1.0 + pre * (1.0 - gate))).astype(BF16)
    rows = lax.broadcasted_iota(jnp.int32, (block_rows, block_rows), 0)
    for j in range(per_step):
        at = slice(j * block_rows, (j + 1) * block_rows)
        pick = (rows == slot[0, :, at]).astype(BF16)
        to = pl.ds(pl.multiple_of(codes[step * per_step + j] * block_rows, block_rows), block_rows)
        total[to, :] += dot(pick, hidden[at])

    @pl.when(step == pl.num_programs(0) - 1)
    def _():
        agg[...] = total[...].astype(BF16)


def edge_backward_kernel(
    block_rows, per_step, codes, lat, send, slot, grads, slope, grad_lat, grad_own, grad_other
):
    step = pl.program_id(0)
    edges = lat.shape[0]
    nodes = grad_own.shape[0]

    @pl.when(step == 0)
    def _():
        grad_lat[...] = jnp.zeros_like(grad_lat)
        grad_own[...] = jnp.zeros_like(grad_own)
        grad_other[...] = jnp.zeros_like(grad_other)

    rows = lax.broadcasted_iota(jnp.int32, (block_rows, block_rows), 0)
    parts = []
    for j in range(per_step):
        at = slice(j * block_rows, (j + 1) * block_rows)
        pick = (rows == slot[0, :, at]).astype(BF16)
        to = pl.ds(pl.multiple_of(codes[step * per_step + j] * block_rows, block_rows), block_rows)
        parts.append((t_dot(pick, grads[to, :]) * slope[at].astype(F32)).astype(BF16))
    grad_pre = jnp.concatenate(parts, axis=0)
    grad_lat[...] += t_dot(lat[...], grad_pre)
    places = lax.broadcasted_iota(jnp.int32, (nodes, edges), 0)
    ids = send[0]
    grad_own[...] += dot((places == ids).astype(BF16), grad_pre)
    grad_other[...] += dot((places + nodes == ids).astype(BF16), grad_pre)


def node_kernel(
    agg, nodes, cot, weo, wni, bn, wno, gain,
    gathered_o, hidden_o, gu_o, gnp_o, gg_o, new_o, cat_o,
):
    latent = nodes.shape[1]
    gathered = dot(agg[...], weo[...]).astype(BF16)
    gathered_o[...] = gathered
    lat = nodes[...]
    pre = dot(lat, wni[:latent]) + dot(gathered, wni[latent:]) + bn[...].astype(F32)
    gate = logistic(pre)
    hidden = (pre * gate).astype(BF16)
    slope = gate * (1.0 + pre * (1.0 - gate))
    hidden_o[...] = hidden
    update = dot(hidden, wno[...])
    scale = gain[...].astype(F32)
    centred = update - jnp.mean(update, axis=-1, keepdims=True)
    inv = lax.rsqrt(jnp.mean(centred * centred, axis=-1, keepdims=True) + 1e-05)
    unit = centred * inv
    new_o[...] = (lat.astype(F32) + unit * scale).astype(BF16)
    cot_gain = cot[...].astype(F32) * scale
    grad = cot_gain - jnp.mean(cot_gain, axis=-1, keepdims=True)
    grad = (grad - unit * jnp.mean(cot_gain * unit, axis=-1, keepdims=True)) * inv
    grad = grad.astype(BF16)
    gu_o[...] = grad
    gnp = (dot_t(grad, wno[...]) * slope).astype(BF16)
    gnp_o[...] = gnp
    cat = dot_t(gnp, wni[...])
    cat_o[...] = cat[:, :latent].astype(BF16)
    gg_o[...] = cat[:, latent:].astype(BF16)


def reduce_kernel(
    regions, value, out, from_sub, shared, half_sum, from_region, piece, gathered,
    sub_send, sub_recv, rs_send, rs_recv, ag_send, ag_recv, share_send, share_recv,
):
    me = lax.axis_index("region")
    sub = lax.axis_index("sub")
    other = 1 - sub
    half = value.shape[0] // 2
    chunk = half // regions
    barrier = pltpu.get_barrier_semaphore()
    pl.semaphore_signal(barrier, inc=1, device_id={"sub": other}, device_id_type=MESH)
    for j in range(1, regions):
        pl.semaphore_signal(
            barrier, inc=1, device_id={"region": lax.rem(me + j, regions)}, device_id_type=MESH
        )
    pl.semaphore_wait(barrier, regions)

    def rows(index, size):
        return pl.ds(pl.multiple_of(index * size, 16), size)

    first = pltpu.make_async_remote_copy(
        value.at[rows(other, half), :], from_sub, sub_send, sub_recv,
        device_id={"sub": other}, device_id_type=MESH,
    )
    first.start()
    first.wait()
    half_sum[...] = (value[rows(sub, half), :].astype(F32) + from_sub[...].astype(F32)).astype(BF16)
    sends = []
    for j in range(1, regions):
        to = lax.rem(me + j, regions)
        copy = pltpu.make_async_remote_copy(
            half_sum.at[rows(to, chunk), :], from_region.at[j], rs_send.at[j], rs_recv.at[j],
            device_id={"region": to}, device_id_type=MESH,
        )
        copy.start()
        sends.append(copy)
    total = half_sum[rows(me, chunk), :].astype(F32)
    for j in range(1, regions):
        sends[j - 1].wait_recv()
        total = total + from_region[j].astype(F32)
    piece[...] = total.astype(BF16)
    gathers = []
    for j in range(1, regions):
        to = lax.rem(me + j, regions)
        copy = pltpu.make_async_remote_copy(
            piece, gathered.at[j], ag_send.at[j], ag_recv.at[j],
            device_id={"region": to}, device_id_type=MESH,
        )
        copy.start()
        gathers.append(copy)
    shares = []
    base = half
    for j in range(regions):
        if j:
            gathers[j - 1].wait_recv()
            source = gathered.at[j]
        else:
            source = piece
        copy = pltpu.make_async_remote_copy(
            source, shared.at[pl.ds(j * chunk, chunk), :], share_send.at[j], share_recv.at[j],
            device_id={"sub": other}, device_id_type=MESH,
        )
        copy.start()
        shares.append(copy)
        origin = lax.rem(me - j + regions, regions)
        out[rows(sub * regions + origin, chunk), :] = source[...].astype(F32)
    for j in range(regions):
        shares[j].wait_recv()
        origin = lax.rem(me - j + regions, regions)
        out[rows(other * regions + origin, chunk), :] = shared[j * chunk:(j + 1) * chunk, :].astype(F32)
    first_done = sends + gathers + shares
    for copy in first_done:
        copy.wait_send()


def reduce_over(value, regions, collective_id):
    half = value.shape[0] // 2
    chunk = half // regions
    width = value.shape[1]
    dma = pltpu.SemaphoreType.DMA
    return pl.pallas_call(
        functools.partial(reduce_kernel, regions),
        out_shape=jax.ShapeDtypeStruct(value.shape, F32),
        in_specs=[pl.BlockSpec(memory_space=pltpu.VMEM)],
        out_specs=pl.BlockSpec(memory_space=pltpu.VMEM),
        scratch_shapes=[
            pltpu.VMEM((half, width), BF16),
            pltpu.VMEM((half, width), BF16),
            pltpu.VMEM((half, width), BF16),
            pltpu.VMEM((regions, chunk, width), BF16),
            pltpu.VMEM((chunk, width), BF16),
            pltpu.VMEM((regions, chunk, width), BF16),
            dma, dma, dma((regions,)), dma((regions,)), dma((regions,)), dma((regions,)),
            dma((regions,)), dma((regions,)),
        ],
        compiler_params=pltpu.CompilerParams(
            collective_id=collective_id, has_side_effects=True, vmem_limit_bytes=VMEM_BYTES
        ),
    )(value)


def on_device(
    edge_lat,
    node_lat,
    senders,
    recv_slots,
    owners,
    targets,
    w_edge_in,
    b_edge,
    w_edge_out,
    w_node_in,
    b_node,
    w_node_out,
    norm_gain,
    cotangent,
):
    regions = lax.axis_size("region")
    me = lax.axis_index("region")
    hid = lax.axis_index("hid")
    sub = lax.axis_index("sub")
    blocks = owners.shape[0]
    edges = edge_lat.shape[0]
    block_rows = edges // blocks
    node_rows, latent = node_lat.shape
    width = w_edge_in.shape[1]
    recv_blocks = node_rows // block_rows
    hids = lax.axis_size("hid")
    share = node_rows // hids
    per_step = 4 if blocks % 4 == 0 else 1
    steps = blocks // per_step
    span = per_step * block_rows

    def swap(value, axis):
        return lax.ppermute(value, axis, [(0, 1), (1, 0)])

    def hid_shift(value, by):
        return lax.ppermute(value, "hid", [(i, (i + by) % hids) for i in range(hids)])

    def hid_all(value, axis=0):
        return jnp.concatenate([value] + [hid_shift(value, j) for j in range(1, hids)], axis=axis)

    def ordered(parts):
        descending = parts[::-1]
        rows = parts[0].shape[0]
        doubled = jnp.concatenate(descending + descending[:-1], axis=0)
        return lax.dynamic_slice_in_dim(doubled, (hids - 1 - hid) * rows, hids * rows, 0)

    def hid_ordered(value):
        return ordered([value] + [hid_shift(value, j) for j in range(1, hids)])

    def hid_sum(value):
        total = value.astype(F32)
        for j in range(1, hids):
            total = total + hid_shift(value, j).astype(F32)
        return total

    def shift(value, by):
        return lax.ppermute(value, "region", [(i, (i + by) % regions) for i in range(regions)])

    weo = hid_all(w_edge_out)
    wni = hid_all(w_node_in, 1)
    wno = hid_all(w_node_out)
    bn = hid_all(b_node)

    own_part = jnp.dot(node_lat, w_edge_in[latent:], preferred_element_type=F32).astype(BF16)
    other_part = swap(own_part, "sub")

    owner = owners[:, 0]
    ahead = lax.rem(owner - me + regions, regions) * recv_blocks + targets
    behind = lax.rem(me - owner + regions, regions) * recv_blocks + targets
    send_rows = jnp.bitwise_xor(senders // node_rows, sub) * node_rows + senders % node_rows
    send_rows = send_rows.reshape(steps, 1, span)
    slots = recv_slots.reshape(steps, 1, span)
    whole = lambda *shape: pl.BlockSpec(shape, lambda i, c: (0,) * len(shape))
    tile = lambda cols: pl.BlockSpec((span, cols), lambda i, c: (i, 0))
    ids = pl.BlockSpec((1, 1, span), lambda i, c: (i, 0, 0))
    params = pltpu.CompilerParams(vmem_limit_bytes=VMEM_BYTES)
    agg_rows = regions * node_rows

    agg, slope = pl.pallas_call(
        functools.partial(edge_forward_kernel, block_rows, per_step),
        out_shape=(
            jax.ShapeDtypeStruct((agg_rows, width), BF16),
            jax.ShapeDtypeStruct((edges, width), BF16),
        ),
        grid_spec=pltpu.PrefetchScalarGridSpec(
            num_scalar_prefetch=1,
            grid=(steps,),
            in_specs=[
                tile(latent), ids, ids, whole(node_rows, width), whole(node_rows, width),
                whole(latent, width), whole(1, width),
            ],
            out_specs=[whole(agg_rows, width), tile(width)],
            scratch_shapes=[pltpu.VMEM((agg_rows, width), F32)],
        ),
        compiler_params=params,
    )(ahead, edge_lat, send_rows, slots, own_part, other_part, w_edge_in[:latent], b_edge[None])

    agg = agg.reshape(regions, node_rows, width)
    gathered_k = agg[0].astype(F32)
    for arrived in [shift(agg[j], j) for j in range(1, regions)]:
        gathered_k = gathered_k + arrived.astype(F32)
    gathered_k = gathered_k.astype(BF16)

    def rows_of(value, by):
        at = lax.rem(hid + by, hids) * share
        return lax.dynamic_slice_in_dim(value, at, share, 0)

    agg_mine = jnp.concatenate(
        [rows_of(gathered_k, 0)]
        + [hid_shift(rows_of(gathered_k, j), j) for j in range(1, hids)],
        axis=1,
    )
    row = lambda cols: jax.ShapeDtypeStruct((share, cols), BF16)
    all_units = hids * width
    gathered, hidden, gu, gnp, gg, new_rows, cat = pl.pallas_call(
        node_kernel,
        out_shape=(
            row(latent), row(all_units), row(latent), row(all_units), row(latent), row(latent),
            row(latent),
        ),
        compiler_params=params,
    )(
        agg_mine, rows_of(node_lat, 0), rows_of(cotangent, 0), weo, wni, bn[None], wno,
        norm_gain[None],
    )
    gg_all = hid_ordered(gg)
    gs = dot_t(gg_all, w_edge_out).astype(BF16)
    gs_all = jnp.concatenate([gs] + [shift(gs, j) for j in range(1, regions)], axis=0)

    new_nodes = hid_ordered(new_rows)
    packs = []
    for j in range(hids):
        at = (hids - j) % hids * width
        pack = jnp.concatenate(
            [gathered, gu, hidden[:, at:at + width], gnp[:, at:at + width]], axis=1
        )
        packs.append(hid_shift(pack, j) if j else pack)
    packed = ordered(packs)
    gathered_all = packed[:, :latent]
    gu_all = packed[:, latent:2 * latent]
    hid_rows = packed[:, 2 * latent:2 * latent + width]
    gnp_all = packed[:, 2 * latent + width:]
    grad_node_in = t_dot(jnp.concatenate([node_lat, gathered_all], axis=1), gnp_all)
    grad_node_out = t_dot(hid_rows, gu_all)
    grad_edge_out = t_dot(gathered_k, gg_all)

    grad_lat, grad_own, grad_other = pl.pallas_call(
        functools.partial(edge_backward_kernel, block_rows, per_step),
        out_shape=(
            jax.ShapeDtypeStruct((latent, width), F32),
            jax.ShapeDtypeStruct((node_rows, width), F32),
            jax.ShapeDtypeStruct((node_rows, width), F32),
        ),
        grid_spec=pltpu.PrefetchScalarGridSpec(
            num_scalar_prefetch=1,
            grid=(steps,),
            in_specs=[tile(latent), ids, ids, whole(agg_rows, width), tile(width)],
            out_specs=[whole(latent, width), whole(node_rows, width), whole(node_rows, width)],
        ),
        compiler_params=params,
    )(behind, edge_lat, send_rows, slots, gs_all, slope)

    grad_send = (grad_own + swap(grad_other.astype(BF16), "sub").astype(F32)).astype(BF16)
    node_part = dot_t(grad_send, w_edge_in[latent:])
    cat_rows = lax.dynamic_update_slice_in_dim(
        jnp.zeros((node_rows, latent), BF16), cat, hid * share, 0
    )
    node_part = (node_part + cat_rows.astype(F32)).astype(BF16)
    grad_nodes = (cotangent.astype(F32) + hid_sum(node_part)).astype(BF16)

    def tall(value):
        value = value.astype(BF16)
        return [value[:, at:at + width] for at in range(0, latent, width)]

    stacked = jnp.concatenate(
        [grad_node_in.astype(BF16)]
        + tall(grad_node_out)
        + tall(grad_edge_out)
        + [grad_lat.astype(BF16), t_dot(node_lat, grad_send).astype(BF16)],
        axis=0,
    )
    reduced = reduce_over(stacked, regions, 1)

    def flat(at):
        return jnp.concatenate(
            [reduced[at + step:at + step + width] for step in range(0, latent, width)], axis=1
        )

    return (
        new_nodes,
        grad_nodes,
        reduced[4 * latent:],
        flat(3 * latent),
        reduced[:2 * latent],
        flat(2 * latent),
    )


def solution(mesh):
    placed = (
        P(("group", "region", "sub"), None),
        P(("group", "region", "sub"), None),
        P(("group", "region", "sub")),
        P(("group", "region", "sub")),
        P(("group", "region", "sub"), None),
        P(("group", "region", "sub")),
        P(None, "hid"),
        P("hid"),
        P("hid", None),
        P(None, "hid"),
        P("hid"),
        P("hid", None),
        P(),
        P(("group", "region", "sub"), None),
    )
    return jax.shard_map(
        on_device,
        mesh=mesh,
        in_specs=placed,
        out_specs=(
            P(("group", "region", "sub"), None),
            P(("group", "region", "sub"), None),
            P("group", "hid"),
            P(("group", "hid"), None),
            P("group", "hid"),
            P(("group", "hid"), None),
        ),
        check_vma=False,
    )
```

```python
import functools
import jax
import jax.numpy as jnp
from jax import lax
from jax.experimental import pallas as pl
from jax.experimental.pallas import tpu as pltpu
from jax.sharding import PartitionSpec as P

F32 = jnp.float32
BF16 = jnp.bfloat16
MESH = pl.DeviceIdType.MESH
VMEM_BYTES = 48 * 1024 * 1024


def dot(a, b):
    return jnp.dot(a, b, preferred_element_type=F32)


def dot_t(a, b):
    return lax.dot_general(a, b, (((1,), (1,)), ((), ())), preferred_element_type=F32)


def t_dot(a, b):
    return lax.dot_general(a, b, (((0,), (0,)), ((), ())), preferred_element_type=F32)


def logistic(v):
    return 1.0 / (1.0 + jnp.exp(-v))


def edge_forward_kernel(
    block_rows, per_step, codes, lat, send, slot, own_part, other_part, w_lat, bias, agg, slope, total
):
    step = pl.program_id(0)
    edges = lat.shape[0]
    nodes = own_part.shape[0]

    @pl.when(step == 0)
    def _():
        total[...] = jnp.zeros_like(total)

    places = lax.broadcasted_iota(jnp.int32, (nodes, edges), 0)
    ids = send[0]
    pre = dot(lat[...], w_lat[...]) + bias[...].astype(F32)
    pre += t_dot((places == ids).astype(BF16), own_part[...])
    pre += t_dot((places + nodes == ids).astype(BF16), other_part[...])
    gate = logistic(pre)
    hidden = (pre * gate).astype(BF16)
    slope[...] = (gate * (1.0 + pre * (1.0 - gate))).astype(BF16)
    rows = lax.broadcasted_iota(jnp.int32, (block_rows, block_rows), 0)
    for j in range(per_step):
        at = slice(j * block_rows, (j + 1) * block_rows)
        pick = (rows == slot[0, :, at]).astype(BF16)
        to = pl.ds(pl.multiple_of(codes[step * per_step + j] * block_rows, block_rows), block_rows)
        total[to, :] += dot(pick, hidden[at])

    @pl.when(step == pl.num_programs(0) - 1)
    def _():
        agg[...] = total[...].astype(BF16)


def core_kernel(regions, hids, blocks, per_step, *refs):
    refs = list(refs)

    def take(count):
        got = refs[:count]
        del refs[:count]
        return got

    agg, nodes, cot, gain, w_send, edge_hbm, slope_hbm, send, cell = take(9)
    weo, wni, bn, wno = take(hids), take(hids), take(hids), take(hids)
    new_o, grad_nodes_o, gei_o, geo_o, gni_o, gno_o = take(6)
    edge_v, slope_v, from_region, gk, agg_mine, hidden, gnp = take(7)
    gg_all, gathered_all, gu_all, hid_all, gnp_all, new_all = take(6)
    gs_all, sent_part, own_part, other_part, lat_part, sub_part, node_part, node_parts = take(8)
    stack1, from_sub1, shared1, half1, arrived1, piece1, whole1 = take(7)
    stack2, from_sub2, shared2, half2, arrived2, piece2, whole2, result = take(8)
    local_sem, region_sems, hid_sems, sub_sems, red1_sems, red2_sems = take(6)

    me = lax.axis_index("region")
    hid = lax.axis_index("hid")
    sub = lax.axis_index("sub")
    other = 1 - sub
    count, latent = nodes.shape
    width = gk.shape[1]
    share = count // hids
    block_rows = edge_v.shape[0] // blocks
    span = per_step * block_rows

    fetch = [
        pltpu.make_async_copy(edge_hbm, edge_v, local_sem.at[0]),
        pltpu.make_async_copy(slope_hbm, slope_v, local_sem.at[1]),
    ]
    for copy in fetch:
        copy.start()
    barrier = pltpu.get_barrier_semaphore()
    pl.semaphore_signal(barrier, inc=1, device_id={"sub": other}, device_id_type=MESH)
    for j in range(1, regions):
        pl.semaphore_signal(
            barrier, inc=1, device_id={"region": lax.rem(me + j, regions)}, device_id_type=MESH
        )
    for j in range(1, hids):
        pl.semaphore_signal(
            barrier, inc=1, device_id={"hid": lax.rem(hid + j, hids)}, device_id_type=MESH
        )
    pl.semaphore_wait(barrier, regions + hids - 1)
    started = []

    def push(source, target, sems, index, device):
        copy = pltpu.make_async_remote_copy(
            source, target, sems.at[0, index], sems.at[1, index],
            device_id=device, device_id_type=MESH,
        )
        copy.start()
        started.append(copy)
        return copy

    def to_region(j):
        return {"region": lax.rem(me + j, regions)}

    def to_hid(j):
        return {"hid": lax.rem(hid + j, hids)}

    def rows(index, size):
        return pl.ds(pl.multiple_of(index * size, 16), size)

    def hid_push(kind, source, target):
        return [
            push(source(j), target(j), hid_sems, kind * hids + j, to_hid(j))
            for j in range(1, hids)
        ]

    def arrive(copies):
        for copy in copies:
            copy.wait_recv()

    copies = [
        push(agg.at[j], from_region.at[j], region_sems, j, to_region(j)) for j in range(1, regions)
    ]
    my_rows = rows(hid, share)
    lat = nodes[my_rows, :]
    pre_lat = [dot(lat, wni[j][:latent, :]) + bn[j][...].astype(F32) for j in range(hids)]
    total = agg[0].astype(F32)
    for j in range(1, regions):
        copies[j - 1].wait_recv()
        total = total + from_region[j].astype(F32)
    gk[...] = total.astype(BF16)
    copies = hid_push(
        0, lambda j: gk.at[rows(lax.rem(hid + j, hids), share), :], lambda j: agg_mine.at[j]
    )
    agg_own = gk[my_rows, :]
    gathered = dot(agg_own, weo[0][...])
    for j in range(1, hids):
        copies[j - 1].wait_recv()
        gathered = gathered + dot(agg_mine[j], weo[j][...])
    gathered = gathered.astype(BF16)
    gathered_all[my_rows, :] = gathered

    slopes = []
    update = None
    for j in range(hids):
        pre = pre_lat[j] + dot(gathered, wni[j][latent:, :])
        gate = logistic(pre)
        units = (pre * gate).astype(BF16)
        hidden[j] = units
        slopes.append(gate * (1.0 + pre * (1.0 - gate)))
        term = dot(units, wno[j][...])
        update = term if update is None else update + term
    scale = gain[...].astype(F32)
    centred = update - jnp.mean(update, axis=-1, keepdims=True)
    inv = lax.rsqrt(jnp.mean(centred * centred, axis=-1, keepdims=True) + 1e-05)
    unit = centred * inv
    cot_gain = cot[my_rows, :].astype(F32) * scale
    grad = cot_gain - jnp.mean(cot_gain, axis=-1, keepdims=True)
    grad = (grad - unit * jnp.mean(cot_gain * unit, axis=-1, keepdims=True)) * inv
    grad = grad.astype(BF16)
    gu_all[my_rows, :] = grad
    gg = None
    for j in range(hids):
        units = (dot_t(grad, wno[j][...]) * slopes[j]).astype(BF16)
        gnp[j] = units
        term = dot_t(units, wni[j][latent:, :])
        gg = term if gg is None else gg + term
    gg_all[my_rows, :] = gg.astype(BF16)
    gg_copies = hid_push(1, lambda j: gg_all.at[my_rows, :], lambda j: gg_all.at[my_rows, :])
    new_all[my_rows, :] = (lat.astype(F32) + unit * scale).astype(BF16)
    hid_all[my_rows, :] = hidden[0]
    gnp_all[my_rows, :] = gnp[0]
    back = lambda j: (hids - j) % hids
    pack = hid_push(2, lambda j: gnp.at[back(j)], lambda j: gnp_all.at[my_rows, :])
    pack += hid_push(3, lambda j: hidden.at[back(j)], lambda j: hid_all.at[my_rows, :])
    pack += hid_push(4, lambda j: gathered_all.at[my_rows, :], lambda j: gathered_all.at[my_rows, :])
    pack += hid_push(5, lambda j: gu_all.at[my_rows, :], lambda j: gu_all.at[my_rows, :])
    new_copies = hid_push(6, lambda j: new_all.at[my_rows, :], lambda j: new_all.at[my_rows, :])
    arrive(gg_copies)
    gs_all[:count, :] = dot_t(gg_all[...], weo[0][...]).astype(BF16)
    gs_copies = [
        push(
            gs_all.at[pl.ds(0, count), :], gs_all.at[pl.ds(j * count, count), :],
            region_sems, regions + j, to_region(j),
        )
        for j in range(1, regions)
    ]

    def reducer(stack, from_sub, shared, half_sum, arrived, piece, whole, sems, base):
        half = half_sum.shape[0]
        chunk = half // regions
        held = {}

        def begin():
            held["sub"] = push(
                stack.at[rows(other, half), :], from_sub, sems, 0, {"sub": other}
            )

        def scatter():
            held["sub"].wait_recv()
            half_sum[...] = (
                stack[rows(sub, half), :].astype(F32) + from_sub[...].astype(F32)
            ).astype(BF16)
            held["rs"] = [
                push(
                    half_sum.at[rows(lax.rem(me + j, regions), chunk), :], arrived.at[j],
                    sems, j, to_region(j),
                )
                for j in range(1, regions)
            ]

        def give(source, j):
            target = shared.at[pl.ds(j * chunk, chunk), :]
            held["share"].append(
                push(source, target, sems, 2 * regions + j, {"sub": other})
            )
            origin = lax.rem(me - j + regions, regions)
            result[rows(base // chunk + sub * regions + origin, chunk), :] = source[...].astype(F32)

        def gather():
            total = half_sum[rows(me, chunk), :].astype(F32)
            for j in range(1, regions):
                held["rs"][j - 1].wait_recv()
                total = total + arrived[j].astype(F32)
            piece[...] = total.astype(BF16)
            held["ag"] = [
                push(piece, whole.at[j], sems, regions + j, to_region(j))
                for j in range(1, regions)
            ]
            held["share"] = []
            give(piece, 0)

        def spread():
            for j in range(1, regions):
                held["ag"][j - 1].wait_recv()
                give(whole.at[j], j)

        def finish():
            for j in range(regions):
                held["share"][j].wait_recv()
                origin = lax.rem(me - j + regions, regions)
                result[rows(base // chunk + other * regions + origin, chunk), :] = shared[
                    j * chunk:(j + 1) * chunk, :
                ].astype(F32)

        return begin, scatter, gather, spread, finish

    begin1, scatter1, gather1, spread1, finish1 = reducer(
        stack1, from_sub1, shared1, half1, arrived1, piece1, whole1, red1_sems, 0
    )
    begin2, scatter2, gather2, spread2, finish2 = reducer(
        stack2, from_sub2, shared2, half2, arrived2, piece2, whole2, red2_sems, 4 * latent
    )

    edge_out = t_dot(gk[...], gg_all[...]).astype(BF16)
    arrive(pack)
    units = gnp_all[...]
    stack1[:latent, :] = t_dot(nodes[...], units).astype(BF16)
    stack1[latent:2 * latent, :] = t_dot(gathered_all[...], units).astype(BF16)
    node_out = t_dot(hid_all[...], gu_all[...]).astype(BF16)
    for at in range(0, latent, width):
        stack1[2 * latent + at:2 * latent + at + width, :] = node_out[:, at:at + width]
        stack1[3 * latent + at:3 * latent + at + width, :] = edge_out[:, at:at + width]
    begin1()
    cat = None
    for j in range(hids):
        term = dot_t(gnp[j], wni[j][:latent, :])
        cat = term if cat is None else cat + term
    sent_part[...] = jnp.zeros_like(sent_part)
    sent_part[my_rows, :] = cat
    arrive(new_copies)
    new_o[...] = new_all[...]
    scatter1()

    for copy in fetch:
        copy.wait()
    lat_part[...] = jnp.zeros_like(lat_part)
    own_part[...] = jnp.zeros_like(own_part)
    other_part[...] = jnp.zeros_like(other_part)
    arrive(gs_copies)
    places = lax.broadcasted_iota(jnp.int32, (count, span), 0)
    cells = lax.broadcasted_iota(jnp.int32, (gs_all.shape[0], span), 0)

    def edge_step(step, carry):
        ids = send[step]
        at = pl.ds(pl.multiple_of(step * span, 16), span)
        grad_hidden = t_dot((cells == cell[step]).astype(BF16), gs_all[...])
        grad_pre = (grad_hidden * slope_v[at, :].astype(F32)).astype(BF16)
        lat_part[...] += t_dot(edge_v[at, :], grad_pre)
        own_part[...] += dot((places == ids).astype(BF16), grad_pre)
        other_part[...] += dot((places + count == ids).astype(BF16), grad_pre)
        return carry

    lax.fori_loop(0, blocks // per_step, edge_step, 0)
    sub_part[0] = other_part[...].astype(BF16)
    sub_copy = push(sub_part.at[0], sub_part.at[1], sub_sems, 0, {"sub": other})
    stack2[:latent, :] = lat_part[...].astype(BF16)
    gather1()
    sub_copy.wait_recv()
    grad_send = (own_part[...] + sub_part[1].astype(F32)).astype(BF16)
    stack2[latent:, :] = t_dot(nodes[...], grad_send).astype(BF16)
    begin2()
    node_part[...] = (sent_part[...] + dot_t(grad_send, w_send[...])).astype(BF16)
    part_copies = hid_push(7, lambda j: node_part, lambda j: node_parts.at[j])
    scatter2()
    spread1()
    gather2()
    total = cot[...].astype(F32) + node_part[...].astype(F32)
    for j in range(1, hids):
        part_copies[j - 1].wait_recv()
        total = total + node_parts[j].astype(F32)
    grad_nodes_o[...] = total.astype(BF16)
    finish1()
    gni_o[...] = result[:2 * latent, :]
    for at in range(0, latent, width):
        gno_o[:, at:at + width] = result[2 * latent + at:2 * latent + at + width, :]
        geo_o[:, at:at + width] = result[3 * latent + at:3 * latent + at + width, :]
    spread2()
    finish2()
    gei_o[...] = result[4 * latent:, :]
    for copy in started:
        copy.wait_send()


def on_device(
    edge_lat,
    node_lat,
    senders,
    recv_slots,
    owners,
    targets,
    w_edge_in,
    b_edge,
    w_edge_out,
    w_node_in,
    b_node,
    w_node_out,
    norm_gain,
    cotangent,
):
    regions = lax.axis_size("region")
    me = lax.axis_index("region")
    sub = lax.axis_index("sub")
    blocks = owners.shape[0]
    edges = edge_lat.shape[0]
    block_rows = edges // blocks
    node_rows, latent = node_lat.shape
    width = w_edge_in.shape[1]
    recv_blocks = node_rows // block_rows
    hids = lax.axis_size("hid")
    share = node_rows // hids
    per_step = 4 if blocks % 4 == 0 else 1
    steps = blocks // per_step
    span = per_step * block_rows

    def swap(value, axis):
        return lax.ppermute(value, axis, [(0, 1), (1, 0)])

    def hid_shift(value, by):
        return lax.ppermute(value, "hid", [(i, (i + by) % hids) for i in range(hids)])

    def hid_all(value):
        return [value] + [hid_shift(value, j) for j in range(1, hids)]

    weo = hid_all(w_edge_out)
    wni = hid_all(w_node_in)
    wno = hid_all(w_node_out)
    bn = hid_all(b_node[None])

    own_part = jnp.dot(node_lat, w_edge_in[latent:], preferred_element_type=F32).astype(BF16)
    other_part = swap(own_part, "sub")

    owner = owners[:, 0]
    ahead = lax.rem(owner - me + regions, regions) * recv_blocks + targets
    behind = lax.rem(me - owner + regions, regions) * recv_blocks + targets
    cell = behind[:, None] * block_rows + recv_slots.reshape(blocks, block_rows)
    send_rows = jnp.bitwise_xor(senders // node_rows, sub) * node_rows + senders % node_rows
    send_rows = send_rows.reshape(steps, 1, span)
    slots = recv_slots.reshape(steps, 1, span)
    cell = cell.reshape(steps, 1, span)
    whole = lambda *shape: pl.BlockSpec(shape, lambda i, c: (0,) * len(shape))
    tile = lambda cols: pl.BlockSpec((span, cols), lambda i, c: (i, 0))
    ids = pl.BlockSpec((1, 1, span), lambda i, c: (i, 0, 0))
    params = pltpu.CompilerParams(vmem_limit_bytes=VMEM_BYTES)
    agg_rows = regions * node_rows

    agg, slope = pl.pallas_call(
        functools.partial(edge_forward_kernel, block_rows, per_step),
        out_shape=(
            jax.ShapeDtypeStruct((agg_rows, width), BF16),
            jax.ShapeDtypeStruct((edges, width), BF16),
        ),
        grid_spec=pltpu.PrefetchScalarGridSpec(
            num_scalar_prefetch=1,
            grid=(steps,),
            in_specs=[
                tile(latent), ids, ids, whole(node_rows, width), whole(node_rows, width),
                whole(latent, width), whole(1, width),
            ],
            out_specs=[whole(agg_rows, width), tile(width)],
            scratch_shapes=[pltpu.VMEM((agg_rows, width), F32)],
        ),
        compiler_params=params,
    )(ahead, edge_lat, send_rows, slots, own_part, other_part, w_edge_in[:latent], b_edge[None])

    agg = agg.reshape(regions, node_rows, width)
    vmem = pl.BlockSpec(memory_space=pltpu.VMEM)
    hbm = pl.BlockSpec(memory_space=pl.ANY)
    dma = pltpu.SemaphoreType.DMA
    low = lambda *shape: pltpu.VMEM(shape, BF16)
    high = lambda *shape: pltpu.VMEM(shape, F32)

    def reduce_scratch(height):
        half = height // 2
        chunk = half // regions
        return [
            low(height, width), low(half, width), low(half, width), low(half, width),
            low(regions, chunk, width), low(chunk, width), low(regions, chunk, width),
        ]

    return pl.pallas_call(
        functools.partial(core_kernel, regions, hids, blocks, per_step),
        out_shape=(
            jax.ShapeDtypeStruct((node_rows, latent), BF16),
            jax.ShapeDtypeStruct((node_rows, latent), BF16),
            jax.ShapeDtypeStruct((2 * latent, width), F32),
            jax.ShapeDtypeStruct((width, latent), F32),
            jax.ShapeDtypeStruct((2 * latent, width), F32),
            jax.ShapeDtypeStruct((width, latent), F32),
        ),
        in_specs=[vmem] * 5 + [hbm] * 2 + [vmem] * (2 + 4 * hids),
        out_specs=(vmem,) * 6,
        scratch_shapes=[
            low(edges, latent), low(edges, width), low(regions, node_rows, width),
            low(node_rows, width), low(hids, share, width), low(hids, share, width),
            low(hids, share, width),
            low(node_rows, latent), low(node_rows, latent), low(node_rows, latent),
            low(node_rows, width), low(node_rows, width), low(node_rows, latent),
            low(agg_rows, width), high(node_rows, latent), high(node_rows, width),
            high(node_rows, width), high(latent, width), low(2, node_rows, width),
            low(node_rows, latent), low(hids, node_rows, latent),
            *reduce_scratch(4 * latent),
            *reduce_scratch(2 * latent),
            high(6 * latent, width),
            dma((2,)), dma((2, 2 * regions)), dma((2, 8 * hids)), dma((2, 1)),
            dma((2, 3 * regions)), dma((2, 3 * regions)),
        ],
        compiler_params=pltpu.CompilerParams(
            collective_id=1, has_side_effects=True, vmem_limit_bytes=VMEM_BYTES
        ),
    )(
        agg, node_lat, cotangent, norm_gain[None], w_edge_in[latent:], edge_lat, slope,
        send_rows, cell, *weo, *wni, *bn, *wno,
    )


def solution(mesh):
    placed = (
        P(("group", "region", "sub"), None),
        P(("group", "region", "sub"), None),
        P(("group", "region", "sub")),
        P(("group", "region", "sub")),
        P(("group", "region", "sub"), None),
        P(("group", "region", "sub")),
        P(None, "hid"),
        P("hid"),
        P("hid", None),
        P(None, "hid"),
        P("hid"),
        P("hid", None),
        P(),
        P(("group", "region", "sub"), None),
    )
    return jax.shard_map(
        on_device,
        mesh=mesh,
        in_specs=placed,
        out_specs=(
            P(("group", "region", "sub"), None),
            P(("group", "region", "sub"), None),
            P("group", "hid"),
            P(("group", "hid"), None),
            P("group", "hid"),
            P(("group", "hid"), None),
        ),
        check_vma=False,
    )
```

```python
import functools
import jax
import jax.numpy as jnp
from jax import lax
from jax.experimental import pallas as pl
from jax.experimental.pallas import tpu as pltpu
from jax.sharding import PartitionSpec as P

F32 = jnp.float32
BF16 = jnp.bfloat16
MESH = pl.DeviceIdType.MESH
VMEM_BYTES = 48 * 1024 * 1024


def dot(a, b):
    return jnp.dot(a, b, preferred_element_type=F32)


def dot_t(a, b):
    return lax.dot_general(a, b, (((1,), (1,)), ((), ())), preferred_element_type=F32)


def t_dot(a, b):
    return lax.dot_general(a, b, (((0,), (0,)), ((), ())), preferred_element_type=F32)


def logistic(v):
    return 1.0 / (1.0 + jnp.exp(-v))


def edge_forward_kernel(
    block_rows, per_step, codes, lat, send, slot, own_part, other_part, w_lat, bias, agg, slope, total
):
    step = pl.program_id(0)
    edges = lat.shape[0]
    nodes = own_part.shape[0]

    @pl.when(step == 0)
    def _():
        total[...] = jnp.zeros_like(total)

    places = lax.broadcasted_iota(jnp.int32, (nodes, edges), 0)
    ids = send[0]
    pre = dot(lat[...], w_lat[...]) + bias[...].astype(F32)
    pre += t_dot((places == ids).astype(BF16), own_part[...])
    pre += t_dot((places + nodes == ids).astype(BF16), other_part[...])
    gate = logistic(pre)
    hidden = (pre * gate).astype(BF16)
    slope[...] = (gate * (1.0 + pre * (1.0 - gate))).astype(BF16)
    rows = lax.broadcasted_iota(jnp.int32, (block_rows, block_rows), 0)
    for j in range(per_step):
        at = slice(j * block_rows, (j + 1) * block_rows)
        pick = (rows == slot[0, :, at]).astype(BF16)
        to = pl.ds(pl.multiple_of(codes[step * per_step + j] * block_rows, block_rows), block_rows)
        total[to, :] += dot(pick, hidden[at])

    @pl.when(step == pl.num_programs(0) - 1)
    def _():
        agg[...] = total[...].astype(BF16)


def core_kernel(regions, hids, blocks, per_step, *refs):
    refs = list(refs)

    def take(count):
        got = refs[:count]
        del refs[:count]
        return got

    agg, nodes, cot, gain, w_send, edge_hbm, slope_hbm, send, cell = take(9)
    weo, wni, bn, wno = take(hids), take(1), take(hids), take(hids)
    new_o, grad_nodes_o, gei_o, geo_o, gni_o, gno_o = take(6)
    edge_v, slope_v, from_region, gk, agg_mine, hidden, gnp = take(7)
    gg_all, gathered_all, gu_all, hid_all, gnp_all, new_all = take(6)
    gs_all, sent_part, own_part, other_part, lat_part, sub_part, node_part, node_parts = take(8)
    stack1, from_sub1, shared1, half1, arrived1, piece1, whole1 = take(7)
    stack2, from_sub2, shared2, half2, arrived2, piece2, whole2, result = take(8)
    wni_all, local_sem, region_sems, hid_sems, sub_sems, red1_sems, red2_sems = take(7)
    wni += [wni_all.at[j] for j in range(1, hids)]

    me = lax.axis_index("region")
    hid = lax.axis_index("hid")
    sub = lax.axis_index("sub")
    other = 1 - sub
    count, latent = nodes.shape
    width = gk.shape[1]
    share = count // hids
    block_rows = edge_v.shape[0] // blocks
    span = per_step * block_rows

    fetch = [
        pltpu.make_async_copy(edge_hbm, edge_v, local_sem.at[0]),
        pltpu.make_async_copy(slope_hbm, slope_v, local_sem.at[1]),
    ]
    for copy in fetch:
        copy.start()
    barrier = pltpu.get_barrier_semaphore()
    pl.semaphore_signal(barrier, inc=1, device_id={"sub": other}, device_id_type=MESH)
    for j in range(1, regions):
        pl.semaphore_signal(
            barrier, inc=1, device_id={"region": lax.rem(me + j, regions)}, device_id_type=MESH
        )
    for j in range(1, hids):
        pl.semaphore_signal(
            barrier, inc=1, device_id={"hid": lax.rem(hid + j, hids)}, device_id_type=MESH
        )
    pl.semaphore_wait(barrier, regions + hids - 1)
    started = []

    def push(source, target, sems, index, device):
        copy = pltpu.make_async_remote_copy(
            source, target, sems.at[0, index], sems.at[1, index],
            device_id=device, device_id_type=MESH,
        )
        copy.start()
        started.append(copy)
        return copy

    def to_region(j):
        return {"region": lax.rem(me + j, regions)}

    def to_hid(j):
        return {"hid": lax.rem(hid + j, hids)}

    def rows(index, size):
        return pl.ds(pl.multiple_of(index * size, 16), size)

    def hid_push(kind, source, target):
        return [
            push(source(j), target(j), hid_sems, kind * hids + j, to_hid(j))
            for j in range(1, hids)
        ]

    def arrive(copies):
        for copy in copies:
            copy.wait_recv()

    copies = [
        push(agg.at[j], from_region.at[j], region_sems, j, to_region(j)) for j in range(1, regions)
    ]
    my_rows = rows(hid, share)
    lat = nodes[my_rows, :]
    weight_copies = hid_push(8, lambda j: wni[0], lambda j: wni_all.at[j])
    total = agg[0].astype(F32)
    for j in range(1, regions):
        copies[j - 1].wait_recv()
        total = total + from_region[j].astype(F32)
    gk[...] = total.astype(BF16)
    copies = hid_push(
        0, lambda j: gk.at[rows(lax.rem(hid + j, hids), share), :], lambda j: agg_mine.at[j]
    )
    agg_own = gk[my_rows, :]
    gathered = dot(agg_own, weo[0][...])
    for j in range(1, hids):
        copies[j - 1].wait_recv()
        gathered = gathered + dot(agg_mine[j], weo[j][...])
    gathered = gathered.astype(BF16)
    gathered_all[my_rows, :] = gathered

    arrive(weight_copies)
    pre_lat = [dot(lat, wni[j][:latent, :]) + bn[j][...].astype(F32) for j in range(hids)]
    slopes = []
    update = None
    for j in range(hids):
        pre = pre_lat[j] + dot(gathered, wni[j][latent:, :])
        gate = logistic(pre)
        units = (pre * gate).astype(BF16)
        hidden[j] = units
        slopes.append(gate * (1.0 + pre * (1.0 - gate)))
        term = dot(units, wno[j][...])
        update = term if update is None else update + term
    scale = gain[...].astype(F32)
    centred = update - jnp.mean(update, axis=-1, keepdims=True)
    inv = lax.rsqrt(jnp.mean(centred * centred, axis=-1, keepdims=True) + 1e-05)
    unit = centred * inv
    cot_gain = cot[my_rows, :].astype(F32) * scale
    grad = cot_gain - jnp.mean(cot_gain, axis=-1, keepdims=True)
    grad = (grad - unit * jnp.mean(cot_gain * unit, axis=-1, keepdims=True)) * inv
    grad = grad.astype(BF16)
    gu_all[my_rows, :] = grad
    gg = None
    for j in range(hids):
        units = (dot_t(grad, wno[j][...]) * slopes[j]).astype(BF16)
        gnp[j] = units
        term = dot_t(units, wni[j][latent:, :])
        gg = term if gg is None else gg + term
    gg_all[my_rows, :] = gg.astype(BF16)
    gg_copies = hid_push(1, lambda j: gg_all.at[my_rows, :], lambda j: gg_all.at[my_rows, :])
    new_all[my_rows, :] = (lat.astype(F32) + unit * scale).astype(BF16)
    hid_all[my_rows, :] = hidden[0]
    gnp_all[my_rows, :] = gnp[0]
    back = lambda j: (hids - j) % hids
    pack = hid_push(2, lambda j: gnp.at[back(j)], lambda j: gnp_all.at[my_rows, :])
    pack += hid_push(3, lambda j: hidden.at[back(j)], lambda j: hid_all.at[my_rows, :])
    pack += hid_push(4, lambda j: gathered_all.at[my_rows, :], lambda j: gathered_all.at[my_rows, :])
    pack += hid_push(5, lambda j: gu_all.at[my_rows, :], lambda j: gu_all.at[my_rows, :])
    new_copies = hid_push(6, lambda j: new_all.at[my_rows, :], lambda j: new_all.at[my_rows, :])
    arrive(gg_copies)
    gs_all[:count, :] = dot_t(gg_all[...], weo[0][...]).astype(BF16)
    gs_copies = [
        push(
            gs_all.at[pl.ds(0, count), :], gs_all.at[pl.ds(j * count, count), :],
            region_sems, regions + j, to_region(j),
        )
        for j in range(1, regions)
    ]

    def reducer(stack, from_sub, shared, half_sum, arrived, piece, whole, sems, base):
        half = half_sum.shape[0]
        chunk = half // regions
        held = {}

        def begin():
            held["sub"] = push(
                stack.at[rows(other, half), :], from_sub, sems, 0, {"sub": other}
            )

        def scatter():
            held["sub"].wait_recv()
            half_sum[...] = (
                stack[rows(sub, half), :].astype(F32) + from_sub[...].astype(F32)
            ).astype(BF16)
            held["rs"] = [
                push(
                    half_sum.at[rows(lax.rem(me + j, regions), chunk), :], arrived.at[j],
                    sems, j, to_region(j),
                )
                for j in range(1, regions)
            ]

        def give(source, j):
            target = shared.at[pl.ds(j * chunk, chunk), :]
            held["share"].append(
                push(source, target, sems, 2 * regions + j, {"sub": other})
            )
            origin = lax.rem(me - j + regions, regions)
            result[rows(base // chunk + sub * regions + origin, chunk), :] = source[...].astype(F32)

        def gather():
            total = half_sum[rows(me, chunk), :].astype(F32)
            for j in range(1, regions):
                held["rs"][j - 1].wait_recv()
                total = total + arrived[j].astype(F32)
            piece[...] = total.astype(BF16)
            held["ag"] = [
                push(piece, whole.at[j], sems, regions + j, to_region(j))
                for j in range(1, regions)
            ]
            held["share"] = []
            give(piece, 0)

        def spread():
            for j in range(1, regions):
                held["ag"][j - 1].wait_recv()
                give(whole.at[j], j)

        def finish():
            for j in range(regions):
                held["share"][j].wait_recv()
                origin = lax.rem(me - j + regions, regions)
                result[rows(base // chunk + other * regions + origin, chunk), :] = shared[
                    j * chunk:(j + 1) * chunk, :
                ].astype(F32)

        return begin, scatter, gather, spread, finish

    begin1, scatter1, gather1, spread1, finish1 = reducer(
        stack1, from_sub1, shared1, half1, arrived1, piece1, whole1, red1_sems, 0
    )
    begin2, scatter2, gather2, spread2, finish2 = reducer(
        stack2, from_sub2, shared2, half2, arrived2, piece2, whole2, red2_sems, 4 * latent
    )

    edge_out = t_dot(gk[...], gg_all[...]).astype(BF16)
    arrive(pack)
    units = gnp_all[...]
    stack1[:latent, :] = t_dot(nodes[...], units).astype(BF16)
    stack1[latent:2 * latent, :] = t_dot(gathered_all[...], units).astype(BF16)
    node_out = t_dot(hid_all[...], gu_all[...]).astype(BF16)
    for at in range(0, latent, width):
        stack1[2 * latent + at:2 * latent + at + width, :] = node_out[:, at:at + width]
        stack1[3 * latent + at:3 * latent + at + width, :] = edge_out[:, at:at + width]
    begin1()
    cat = None
    for j in range(hids):
        term = dot_t(gnp[j], wni[j][:latent, :])
        cat = term if cat is None else cat + term
    sent_part[...] = jnp.zeros_like(sent_part)
    sent_part[my_rows, :] = cat
    arrive(new_copies)
    new_o[...] = new_all[...]
    scatter1()

    for copy in fetch:
        copy.wait()
    lat_part[...] = jnp.zeros_like(lat_part)
    own_part[...] = jnp.zeros_like(own_part)
    other_part[...] = jnp.zeros_like(other_part)
    arrive(gs_copies)
    places = lax.broadcasted_iota(jnp.int32, (count, span), 0)
    cells = lax.broadcasted_iota(jnp.int32, (gs_all.shape[0], span), 0)

    def edge_step(step, carry):
        ids = send[step]
        at = pl.ds(pl.multiple_of(step * span, 16), span)
        grad_hidden = t_dot((cells == cell[step]).astype(BF16), gs_all[...])
        grad_pre = (grad_hidden * slope_v[at, :].astype(F32)).astype(BF16)
        lat_part[...] += t_dot(edge_v[at, :], grad_pre)
        own_part[...] += dot((places == ids).astype(BF16), grad_pre)
        other_part[...] += dot((places + count == ids).astype(BF16), grad_pre)
        return carry

    lax.fori_loop(0, blocks // per_step, edge_step, 0)
    sub_part[0] = other_part[...].astype(BF16)
    sub_copy = push(sub_part.at[0], sub_part.at[1], sub_sems, 0, {"sub": other})
    stack2[:latent, :] = lat_part[...].astype(BF16)
    gather1()
    sub_copy.wait_recv()
    grad_send = (own_part[...] + sub_part[1].astype(F32)).astype(BF16)
    stack2[latent:, :] = t_dot(nodes[...], grad_send).astype(BF16)
    begin2()
    node_part[...] = (sent_part[...] + dot_t(grad_send, w_send[...])).astype(BF16)
    part_copies = hid_push(7, lambda j: node_part, lambda j: node_parts.at[j])
    scatter2()
    spread1()
    gather2()
    total = cot[...].astype(F32) + node_part[...].astype(F32)
    for j in range(1, hids):
        part_copies[j - 1].wait_recv()
        total = total + node_parts[j].astype(F32)
    grad_nodes_o[...] = total.astype(BF16)
    finish1()
    gni_o[...] = result[:2 * latent, :]
    for at in range(0, latent, width):
        gno_o[:, at:at + width] = result[2 * latent + at:2 * latent + at + width, :]
        geo_o[:, at:at + width] = result[3 * latent + at:3 * latent + at + width, :]
    spread2()
    finish2()
    gei_o[...] = result[4 * latent:, :]
    for copy in started:
        copy.wait_send()


def on_device(
    edge_lat,
    node_lat,
    senders,
    recv_slots,
    owners,
    targets,
    w_edge_in,
    b_edge,
    w_edge_out,
    w_node_in,
    b_node,
    w_node_out,
    norm_gain,
    cotangent,
):
    regions = lax.axis_size("region")
    me = lax.axis_index("region")
    sub = lax.axis_index("sub")
    blocks = owners.shape[0]
    edges = edge_lat.shape[0]
    block_rows = edges // blocks
    node_rows, latent = node_lat.shape
    width = w_edge_in.shape[1]
    recv_blocks = node_rows // block_rows
    hids = lax.axis_size("hid")
    share = node_rows // hids
    per_step = 4 if blocks % 4 == 0 else 1
    steps = blocks // per_step
    span = per_step * block_rows

    def swap(value, axis):
        return lax.ppermute(value, axis, [(0, 1), (1, 0)])

    def hid_shift(value, by):
        return lax.ppermute(value, "hid", [(i, (i + by) % hids) for i in range(hids)])

    def hid_all(value):
        return [value] + [hid_shift(value, j) for j in range(1, hids)]

    weo = hid_all(w_edge_out)
    wno = hid_all(w_node_out)
    bn = hid_all(b_node[None])

    own_part = jnp.dot(node_lat, w_edge_in[latent:], preferred_element_type=F32).astype(BF16)
    other_part = swap(own_part, "sub")

    owner = owners[:, 0]
    ahead = lax.rem(owner - me + regions, regions) * recv_blocks + targets
    behind = lax.rem(me - owner + regions, regions) * recv_blocks + targets
    cell = behind[:, None] * block_rows + recv_slots.reshape(blocks, block_rows)
    send_rows = jnp.bitwise_xor(senders // node_rows, sub) * node_rows + senders % node_rows
    send_rows = send_rows.reshape(steps, 1, span)
    slots = recv_slots.reshape(steps, 1, span)
    cell = cell.reshape(steps, 1, span)
    whole = lambda *shape: pl.BlockSpec(shape, lambda i, c: (0,) * len(shape))
    tile = lambda cols: pl.BlockSpec((span, cols), lambda i, c: (i, 0))
    ids = pl.BlockSpec((1, 1, span), lambda i, c: (i, 0, 0))
    params = pltpu.CompilerParams(vmem_limit_bytes=VMEM_BYTES)
    agg_rows = regions * node_rows

    agg, slope = pl.pallas_call(
        functools.partial(edge_forward_kernel, block_rows, per_step),
        out_shape=(
            jax.ShapeDtypeStruct((agg_rows, width), BF16),
            jax.ShapeDtypeStruct((edges, width), BF16),
        ),
        grid_spec=pltpu.PrefetchScalarGridSpec(
            num_scalar_prefetch=1,
            grid=(steps,),
            in_specs=[
                tile(latent), ids, ids, whole(node_rows, width), whole(node_rows, width),
                whole(latent, width), whole(1, width),
            ],
            out_specs=[whole(agg_rows, width), tile(width)],
            scratch_shapes=[pltpu.VMEM((agg_rows, width), F32)],
        ),
        compiler_params=params,
    )(ahead, edge_lat, send_rows, slots, own_part, other_part, w_edge_in[:latent], b_edge[None])

    agg = agg.reshape(regions, node_rows, width)
    vmem = pl.BlockSpec(memory_space=pltpu.VMEM)
    hbm = pl.BlockSpec(memory_space=pl.ANY)
    dma = pltpu.SemaphoreType.DMA
    low = lambda *shape: pltpu.VMEM(shape, BF16)
    high = lambda *shape: pltpu.VMEM(shape, F32)

    def reduce_scratch(height):
        half = height // 2
        chunk = half // regions
        return [
            low(height, width), low(half, width), low(half, width), low(half, width),
            low(regions, chunk, width), low(chunk, width), low(regions, chunk, width),
        ]

    return pl.pallas_call(
        functools.partial(core_kernel, regions, hids, blocks, per_step),
        out_shape=(
            jax.ShapeDtypeStruct((node_rows, latent), BF16),
            jax.ShapeDtypeStruct((node_rows, latent), BF16),
            jax.ShapeDtypeStruct((2 * latent, width), F32),
            jax.ShapeDtypeStruct((width, latent), F32),
            jax.ShapeDtypeStruct((2 * latent, width), F32),
            jax.ShapeDtypeStruct((width, latent), F32),
        ),
        in_specs=[vmem] * 5 + [hbm] * 2 + [vmem] * (3 + 3 * hids),
        out_specs=(vmem,) * 6,
        scratch_shapes=[
            low(edges, latent), low(edges, width), low(regions, node_rows, width),
            low(node_rows, width), low(hids, share, width), low(hids, share, width),
            low(hids, share, width),
            low(node_rows, latent), low(node_rows, latent), low(node_rows, latent),
            low(node_rows, width), low(node_rows, width), low(node_rows, latent),
            low(agg_rows, width), high(node_rows, latent), high(node_rows, width),
            high(node_rows, width), high(latent, width), low(2, node_rows, width),
            low(node_rows, latent), low(hids, node_rows, latent),
            *reduce_scratch(4 * latent),
            *reduce_scratch(2 * latent),
            high(6 * latent, width),
            low(hids, 2 * latent, width),
            dma((2,)), dma((2, 2 * regions)), dma((2, 9 * hids)), dma((2, 1)),
            dma((2, 3 * regions)), dma((2, 3 * regions)),
        ],
        compiler_params=pltpu.CompilerParams(
            collective_id=1, has_side_effects=True, vmem_limit_bytes=VMEM_BYTES
        ),
    )(
        agg, node_lat, cotangent, norm_gain[None], w_edge_in[latent:], edge_lat, slope,
        send_rows, cell, *weo, w_node_in, *bn, *wno,
    )


def solution(mesh):
    placed = (
        P(("group", "region", "sub"), None),
        P(("group", "region", "sub"), None),
        P(("group", "region", "sub")),
        P(("group", "region", "sub")),
        P(("group", "region", "sub"), None),
        P(("group", "region", "sub")),
        P(None, "hid"),
        P("hid"),
        P("hid", None),
        P(None, "hid"),
        P("hid"),
        P("hid", None),
        P(),
        P(("group", "region", "sub"), None),
    )
    return jax.shard_map(
        on_device,
        mesh=mesh,
        in_specs=placed,
        out_specs=(
            P(("group", "region", "sub"), None),
            P(("group", "region", "sub"), None),
            P("group", "hid"),
            P(("group", "hid"), None),
            P("group", "hid"),
            P(("group", "hid"), None),
        ),
        check_vma=False,
    )
```
